256 devices in a mesh: grp: 8 (over z), ep: 32 (over x, y, core).
Axes of the slice: x: 4, y: 4, z: 8, core: 2. Of those that a mesh axis runs over, the one named last changes fastest.
Arguments:
- tokens: bfloat16 [8, 1, 1024, 4096], P('grp', None, 'ep'), may hold values from -6 to 6
- gates: float32 [8, 1, 1024, 8], P('grp', None, 'ep'), may hold values from 0.1 to 1
- routes: int32 [8, 1, 1024, 8], P('grp'), may hold values from 0 to 31, all different within a row; in each aligned block of 32 rows (0 to 31, 32 to 63, ..., all dimensions but the last counted through in order) at most 16 rows name the same one
- master_up: float32 [32, 4096, 1536], P('ep', 'grp'), may hold values from -0.09375 to 0.09375
- master_down: float32 [32, 1536, 4096], P('ep', None, 'grp'), may hold values from -0.15625 to 0.15625
Outputs:
- mixed: bfloat16 [8, 1, 1024, 4096], P('grp', None, 'ep')
The draws below stay inside these ranges and needn't reach their ends.
Inputs may be any that keep to these rules, and one draw needn't show every extreme that they name: `routes`: each token names 8 different experts; among the 32 tokens of one aligned block of one group in one step no expert is named more than 16 times, and in some block one expert exactly 16 times.
All inputs are finite; a program needn't handle non-finite values.
Results may differ from the reference program's by a relative error of at most 0.024.
Values may be sent and summed in bfloat16 or wider, within the bound.
No kernel may reach another device: no remote copies, remote signals or barrier semaphores. Data moves between devices by JAX's collectives and lax.ppermute only.
A program may use at most 320 MiB of HBM per device.

```python
import math
import jax
import jax.numpy as jnp
import numpy as np
from jax import lax

D = 4096
FF = 1536
TOP = 8
E = 32
BLK = 128
STEPS = 1
TOK_DEV = 32
CAP = 16
GROUPS = 8
TOKENS = 1024
N_EP = 32


def level_of(rng, dims, shards, smallest, high):
    level, own = 1.0, jax.random.fold_in(rng, 6)
    for dim, blocks in shards:
        steps = jnp.exp(jax.random.uniform(jax.random.fold_in(own, dim), (blocks,), jnp.float32, smallest / len(shards), high / len(shards)))
        level = level * jnp.repeat(steps, dims[dim] // blocks).reshape([-1 if axis == dim else 1 for axis in range(len(dims))])
    return level


def deal_out(key, own, number, rows, count, top, bound, slope):
    ranking = jax.random.permutation(key, count)
    packed, common = shares(count, rows * top, bound, slope, True), shares(count, rows * top, bound, slope, False)
    places = jnp.arange(count)

    def named(tallies, turn):
        used = int((tallies > 0).sum())
        fixed = max(1, used // 4)
        moved = fixed + (places - fixed + turn * (used - fixed)) % max(1, count - fixed)
        return jnp.zeros((count,), jnp.int32).at[ranking[jnp.where(places < fixed, places, moved)]].set(jnp.asarray(tallies, jnp.int32))

    tallies = jnp.where(number % 4 == 0, named(packed, number // 4), named(common, number - number // 4 - 1))
    mixed = jax.random.permutation(jax.random.fold_in(own, 3), count)
    source_of, sink = mixed[0:count // 2 * 2:2], mixed[1:count // 2 * 2:2]
    room = jnp.minimum(tallies[source_of] - 1, bound - tallies[sink]) // 2
    room = jnp.where((source_of == ranking[0]) | (sink == ranking[0]) | (tallies[sink] == 0), 0, jnp.maximum(room, 0))
    moved = jax.random.randint(jax.random.fold_in(own, 4), (count // 2,), 0, 1 << 20) % (room + 1)
    tallies = tallies.at[source_of].add(-moved).at[sink].add(moved)
    labels = jnp.searchsorted(jnp.cumsum(tallies), jnp.arange(rows * top), side="right").astype(jnp.int32)
    table = labels.reshape(top, rows).T
    table = table[jax.random.permutation(jax.random.fold_in(own, 1), rows)]
    turn = jax.random.randint(jax.random.fold_in(own, 2), (rows, 1), 0, top)
    return jnp.take_along_axis(table, (jnp.arange(top)[None, :] + turn) % top, axis=1)


def shares(amount, total, bound, skew, full):
    portions = [(1 << 20) // math.isqrt(rank ** skew) + 1 for rank in range(1, amount + 1)]
    largest = bound if full else min(bound, max(-(-total // amount), total * portions[0] // sum(portions)))
    least = 1 if total - largest >= amount - 1 else 0
    given, spare = [largest] + [least] * (amount - 1), total - largest - least * (amount - 1)
    while spare > 0:
        candidates = [i for i in range(1, amount) if given[i] < largest] or [i for i in range(1, amount) if given[i] < bound]
        whole, remaining = sum([portions[i] for i in candidates]), spare
        for i in candidates:
            extra = min(bound - given[i], max(1, remaining * portions[i] // whole), spare)
            given[i] = given[i] + extra
            spare = spare - extra
    return np.array(given)


def scatter_about(own_key, extent, deviation, most, pieces=(), held_as=jnp.bfloat16):
    gain = level_of(own_key, extent, pieces, -0.22, 0.18) if pieces else 1.0
    entries = jax.random.normal(own_key, extent, jnp.float32) * deviation * gain
    return jnp.minimum(jnp.maximum(entries, -most), most).astype(held_as)


def setup_inputs(seed: int = 0) -> dict:
    key_list = jax.random.split(jax.random.key(seed), 6)
    tokens = scatter_about(key_list[0], (GROUPS, STEPS, TOKENS, D), 1.0, 6.0, ((0, 8), (2, 32)))
    gates = jnp.clip(jnp.exp(math.log(1.0) - 2.3025851 * jax.random.uniform(key_list[1], (GROUPS, STEPS, TOKENS, TOP), jnp.float32) ** level_of(key_list[1], (GROUPS, STEPS, TOKENS, TOP), ((0, 8), (2, 32)), -0.2, 0.2)), 0.1, 1.0)
    routes_keys = jax.random.split(jax.random.fold_in(key_list[2], 1), GROUPS * STEPS * TOKENS // TOK_DEV)
    routes_turns = jax.random.permutation(jax.random.fold_in(key_list[2], 3), GROUPS * STEPS * TOKENS // TOK_DEV)
    routes = jax.vmap(lambda own, number: deal_out(jax.random.fold_in(key_list[2], 2), own, number, TOK_DEV, E, TOP, CAP, 2))(routes_keys, routes_turns).reshape((GROUPS, STEPS, TOKENS, TOP))
    master_up = scatter_about(key_list[3], (E, D, FF), D ** -0.5, 0.09375, ((0, 32), (1, 8)), jnp.float32)
    master_down = scatter_about(key_list[4], (E, FF, D), FF ** -0.5, 0.15625, ((0, 32), (2, 8)), jnp.float32)
    return dict(tokens=tokens, gates=gates, routes=routes, master_up=master_up, master_down=master_down)


def requantize(master):
    count, height, width = master.shape
    blocks = master.reshape(count, height // BLK, BLK, width // BLK, BLK)
    largest = jnp.max(jnp.abs(blocks), axis=(2, 4), keepdims=True)
    scale = (largest / 448.0 + 1e-6).astype(jnp.bfloat16).astype(jnp.float32)
    coded = (blocks / scale).astype(jnp.bfloat16)
    return (coded.astype(jnp.float32) * scale).astype(jnp.bfloat16).reshape(count, height, width)


def slot_rank(route_ids):
    onehot = (route_ids[..., None] == jnp.arange(E, dtype=jnp.int32)).astype(jnp.int32)
    running = jnp.cumsum(onehot, axis=-2)
    return jnp.sum((running - 1) * onehot, axis=-1).astype(jnp.int32)


def run_expert(item):
    rows, up_w, down_w = item
    rows_f = rows.astype(jnp.float32)
    up_acts = jnp.einsum('srd,df->srf', rows_f, up_w.astype(jnp.float32))
    hidden = jax.nn.silu(up_acts).astype(jnp.bfloat16)
    answer = jnp.einsum('srf,fd->srd', hidden.astype(jnp.float32), down_w.astype(jnp.float32))
    return answer.astype(jnp.bfloat16)


def one_group(item, up_w, down_w):
    tokens, gates, routes = item
    route_count = TOK_DEV * TOP
    all_routes = routes.reshape(STEPS, N_EP, route_count)
    ranks = slot_rank(all_routes)
    source_ids = jnp.arange(N_EP, dtype=jnp.int32)[None, :, None]
    slot_pos = (all_routes * N_EP + source_ids) * CAP + ranks
    token_of = source_ids * TOK_DEV + jnp.arange(route_count, dtype=jnp.int32)[None, None, :] // TOP
    step_ids = jnp.arange(STEPS, dtype=jnp.int32)[:, None, None]
    token_of = jnp.broadcast_to(token_of, slot_pos.shape)
    picked_in = tokens[step_ids, token_of]
    buffers = jnp.zeros((STEPS, E * N_EP * CAP, D), jnp.bfloat16).at[step_ids, slot_pos].set(picked_in)
    buffers = buffers.reshape(STEPS, E, N_EP * CAP, D).transpose(1, 0, 2, 3)
    answers = lax.map(run_expert, (buffers, up_w, down_w))
    answers = answers.transpose(1, 0, 2, 3).reshape(STEPS, E * N_EP * CAP, D)
    picked = answers[step_ids, slot_pos].reshape(STEPS, TOKENS, TOP, D)
    mixed = jnp.sum(gates[..., None] * picked.astype(jnp.float32), axis=2)
    return mixed.astype(jnp.bfloat16)


def reference(tokens, gates, routes, master_up, master_down):
    up_w = requantize(master_up)
    down_w = requantize(master_down)
    return lax.map(lambda item: one_group(item, up_w, down_w), (tokens, gates, routes))
```

```python
import jax
import jax.numpy as jnp
from jax import lax
from jax.experimental import pallas as pl
from jax.experimental.pallas import tpu as pltpu
from jax.sharding import PartitionSpec as P

E = 32
BLK = 128
CAP = 16
PARTS = 4


def coded_block(entries):
    largest = jnp.max(jnp.max(jnp.abs(entries), axis=0, keepdims=True), axis=1, keepdims=True)
    scale = (largest / 448.0 + 1e-06).astype(jnp.bfloat16).astype(jnp.float32)
    coded = (entries / scale).astype(jnp.bfloat16)
    return (coded.astype(jnp.float32) * scale).astype(jnp.bfloat16)


def requantize_rows_kernel(master_ref, out_ref):
    for part in range(master_ref.shape[1] // BLK):
        columns = slice(part * BLK, (part + 1) * BLK)
        out_ref[:, columns] = coded_block(master_ref[:, columns])


def requantize_rows(master):
    height, width = master.shape
    return pl.pallas_call(
        requantize_rows_kernel,
        grid=(height // BLK,),
        in_specs=[pl.BlockSpec((BLK, width), lambda i: (i, 0))],
        out_specs=pl.BlockSpec((BLK, width), lambda i: (i, 0)),
        out_shape=jax.ShapeDtypeStruct((height, width), jnp.bfloat16),
        cost_estimate=pl.CostEstimate(
            flops=6 * height * width, bytes_accessed=6 * height * width, transcendentals=0
        ),
        name="requantize_up",
    )(master)


def requantize_columns_kernel(master_ref, *out_refs):
    for row in range(master_ref.shape[0] // BLK):
        rows = slice(row * BLK, (row + 1) * BLK)
        for part, out_ref in enumerate(out_refs):
            out_ref[rows, :] = coded_block(master_ref[rows, part * BLK:(part + 1) * BLK])


def requantize_columns(master):
    height, width = master.shape
    step = 3 * BLK
    return pl.pallas_call(
        requantize_columns_kernel,
        grid=(height // step,),
        in_specs=[pl.BlockSpec((step, width), lambda i: (i, 0))],
        out_specs=[pl.BlockSpec((step, BLK), lambda i: (i, 0))] * (width // BLK),
        out_shape=[jax.ShapeDtypeStruct((height, BLK), jnp.bfloat16)] * (width // BLK),
        cost_estimate=pl.CostEstimate(
            flops=6 * height * width, bytes_accessed=6 * height * width, transcendentals=0
        ),
        name="requantize_down",
    )(master)


def local(tokens, gates, routes, master_up, master_down):
    tokens = tokens[0, 0]
    gates = gates[0, 0]
    routes = routes[0, 0]
    ep_count = lax.axis_size("ep")
    tok_dev, width = tokens.shape
    slot_total = ep_count * CAP

    up_q = requantize_rows(master_up[0])
    up_w = lax.all_gather(up_q, "grp", axis=0, tiled=True)
    down_q = requantize_columns(master_down[0])
    down_w = [lax.all_gather(part, "grp", axis=1, tiled=True) for part in down_q]

    own_routes = lax.dynamic_slice_in_dim(routes, lax.axis_index("ep") * tok_dev, tok_dev, 0)
    named = own_routes[:, :, None] == jnp.arange(E, dtype=jnp.int32)
    mask = jnp.any(named, axis=1)
    gate_of = jnp.sum(jnp.where(named, gates[:, :, None], 0.0), axis=1)
    earlier = jnp.tril(jnp.ones((tok_dev, tok_dev), jnp.bfloat16), -1)
    rank = jnp.dot(earlier, mask.astype(jnp.bfloat16), preferred_element_type=jnp.float32)
    rank = jnp.where(mask, rank.astype(jnp.int32), -1)
    in_slot = rank[:, :, None] == jnp.arange(CAP, dtype=jnp.int32)
    place = in_slot.reshape(tok_dev, slot_total).astype(jnp.bfloat16)
    gate_hi = gate_of.astype(jnp.bfloat16)
    gate_lo = (gate_of - gate_hi.astype(jnp.float32)).astype(jnp.bfloat16)
    weigh = jnp.concatenate(
        [
            jnp.where(in_slot, part[:, :, None], 0.0).astype(jnp.bfloat16).reshape(tok_dev, slot_total)
            for part in (gate_hi, gate_lo)
        ],
        axis=0,
    )

    send = lax.dot_general(place, tokens, (((0,), (0,)), ((), ())), preferred_element_type=jnp.float32)
    send = send.astype(jnp.bfloat16).reshape(ep_count, CAP, width)
    rows = lax.all_to_all(send, "ep", split_axis=0, concat_axis=0, tiled=True).reshape(slot_total, width)

    hidden = jnp.dot(rows, up_w, preferred_element_type=jnp.float32)
    hidden = jax.nn.silu(hidden).astype(jnp.bfloat16)
    hidden = lax.optimization_barrier(hidden)

    pieces = []
    for weights in down_w:
        answer = jnp.dot(hidden, weights, preferred_element_type=jnp.float32).astype(jnp.bfloat16)
        part = answer.shape[1]
        back = lax.all_to_all(
            answer.reshape(ep_count, CAP, part), "ep", split_axis=0, concat_axis=0, tiled=True
        ).reshape(slot_total, part)
        both = jnp.dot(weigh, back, preferred_element_type=jnp.float32)
        mixed = (both[:tok_dev] + both[tok_dev:]).astype(jnp.bfloat16)
        pieces.append(mixed.reshape(tok_dev, -1, 1, BLK))
    return jnp.concatenate(pieces, axis=2).reshape(1, 1, tok_dev, width)


def solution(mesh):
    placed = (
        P("grp", None, "ep", None),
        P("grp", None, "ep", None),
        P("grp", None, None, None),
        P("ep", "grp", None),
        P("ep", None, "grp"),
    )
    return jax.shard_map(
        local, mesh=mesh, in_specs=placed, out_specs=P("grp", None, "ep", None), check_vma=False
    )
```

```python
import jax
import jax.numpy as jnp
from jax import lax
from jax.experimental import pallas as pl
from jax.experimental.pallas import tpu as pltpu
from jax.sharding import PartitionSpec as P

E = 32
BLK = 128
CAP = 16
STREAMS = 4
GROUPS_OF_STEPS = ((0, 1), (2, 3), (4, 5), (6,), (7,))
VMEM = 40 * 1024 * 1024


def coded_block(entries):
    largest = jnp.max(jnp.max(jnp.abs(entries), axis=0, keepdims=True), axis=1, keepdims=True)
    scale = (largest / 448.0 + 1e-06).astype(jnp.bfloat16).astype(jnp.float32)
    coded = (entries / scale).astype(jnp.bfloat16)
    return (coded.astype(jnp.float32) * scale).astype(jnp.bfloat16)


def requantize_kernel(master_ref, *out_refs):
    height, width = master_ref.shape
    share = width // len(out_refs)
    for row in range(height // BLK):
        rows = slice(row * BLK, (row + 1) * BLK)
        for column in range(width // BLK):
            start = column * BLK
            place = start % share
            out_refs[start // share][rows, place:place + BLK] = coded_block(
                master_ref[rows, start:start + BLK]
            )


def requantize(master, step, name):
    height, width = master.shape
    share = width // STREAMS
    return pl.pallas_call(
        requantize_kernel,
        grid=(height // step,),
        in_specs=[pl.BlockSpec((step, width), lambda i: (i, 0))],
        out_specs=[pl.BlockSpec((step, share), lambda i: (i, 0))] * STREAMS,
        out_shape=[jax.ShapeDtypeStruct((height, share), jnp.bfloat16)] * STREAMS,
        cost_estimate=pl.CostEstimate(
            flops=6 * height * width, bytes_accessed=6 * height * width, transcendentals=0
        ),
        name=name,
    )(master)


def up_kernel(steps, first, last, place_ref, *refs):
    count = 2 * len(steps)
    rows = refs[:count]
    weights = refs[count:count + STREAMS * len(steps)]
    rest = refs[count + STREAMS * len(steps):]
    out_ref = rest[-1]
    share = weights[0].shape[1]
    for stream in range(STREAMS):
        columns = slice(stream * share, (stream + 1) * share)
        total = None if first else rest[0][:, columns]
        for turn in range(len(steps)):
            source = rows[2 * turn + (stream >= STREAMS // 2)]
            product = jnp.dot(
                source[...], weights[STREAMS * turn + stream][...], preferred_element_type=jnp.float32
            )
            total = product if total is None else total + product
        if last:
            total = total / (1.0 + jnp.exp(-total))
        out_ref[:, columns] = total.astype(out_ref.dtype)


def up_step(place, rows, slices, total, steps, last):
    count, depth = rows.shape[0], slices[0][0].shape[0]
    share = slices[0][0].shape[1]
    size = rows.shape[1] // depth
    first = total is None
    whole = pl.BlockSpec((count, share * STREAMS), lambda i, place: (0, 0))
    in_specs, operands = [], []
    for step in steps:
        for sign in (-1, 1):
            in_specs.append(
                pl.BlockSpec(
                    (count, depth),
                    lambda i, place, offset=sign * step + size: (0, lax.rem(place[0] + offset, size)),
                )
            )
            operands.append(rows)
    for parts in slices:
        for part in parts:
            in_specs.append(pl.BlockSpec(part.shape, lambda i, place: (0, 0)))
            operands.append(part)
    if not first:
        in_specs.append(whole)
        operands.append(total)
    flops = 2 * count * depth * share * STREAMS * len(steps)
    return pl.pallas_call(
        lambda *refs: up_kernel(steps, first, last, *refs),
        grid_spec=pltpu.PrefetchScalarGridSpec(
            num_scalar_prefetch=1, grid=(1,), in_specs=in_specs, out_specs=whole
        ),
        out_shape=jax.ShapeDtypeStruct(
            (count, share * STREAMS), jnp.bfloat16 if last else jnp.float32
        ),
        input_output_aliases={} if first or last else {len(operands): 0},
        compiler_params=pltpu.CompilerParams(vmem_limit_bytes=VMEM),
        cost_estimate=pl.CostEstimate(
            flops=flops,
            bytes_accessed=8 * 1024 * 1024,
            transcendentals=count * share * STREAMS if last else 0,
        ),
        name="up_step",
    )(place, *operands)


def down_kernel(hidden_ref, *refs):
    out_ref = refs[-1]
    for index, weights in enumerate(refs[:-1]):
        part = weights.shape[1]
        out_ref[:, index * part:(index + 1) * part] = jnp.dot(
            hidden_ref[...], weights[...], preferred_element_type=jnp.float32
        ).astype(out_ref.dtype)


def down_step(hidden, slices):
    parts = [part for one in slices for part in one]
    count, depth = hidden.shape
    width = sum(part.shape[1] for part in parts)
    return pl.pallas_call(
        down_kernel,
        out_shape=jax.ShapeDtypeStruct((count, width), jnp.bfloat16),
        compiler_params=pltpu.CompilerParams(vmem_limit_bytes=VMEM),
        cost_estimate=pl.CostEstimate(
            flops=2 * count * depth * width,
            bytes_accessed=2 * (count * depth + depth * width + count * width),
            transcendentals=0,
        ),
        name="down_step",
    )(hidden, *parts)


def ring(own, before):
    size = lax.axis_size("grp")
    right = [(i, (i + 1) % size) for i in range(size)]
    left = [(i, (i - 1) % size) for i in range(size)]
    held = [own]
    now = own
    if before is not None:
        now = [lax.optimization_barrier((a, b))[0] for a, b in zip(own, before)]
    for _ in range(size - 1):
        now = [
            lax.ppermute(part, "grp", right if stream < STREAMS // 2 else left)
            for stream, part in enumerate(now)
        ]
        held.append(now)
    return held


def local(tokens, gates, routes, master_up, master_down):
    tokens = tokens[0, 0]
    gates = gates[0, 0]
    routes = routes[0, 0]
    ep_count = lax.axis_size("ep")
    size = lax.axis_size("grp")
    tok_dev, width = tokens.shape
    slot_total = ep_count * CAP
    here = lax.axis_index("grp").astype(jnp.int32)

    up = ring(requantize(master_up[0], BLK, "requantize_up"), None)
    down = ring(requantize(master_down[0], 3 * BLK, "requantize_down"), up[-1])

    own_routes = lax.dynamic_slice_in_dim(routes, lax.axis_index("ep") * tok_dev, tok_dev, 0)
    named = own_routes[:, :, None] == jnp.arange(E, dtype=jnp.int32)
    mask = jnp.any(named, axis=1)
    gate_of = jnp.sum(jnp.where(named, gates[:, :, None], 0.0), axis=1)
    earlier = jnp.tril(jnp.ones((tok_dev, tok_dev), jnp.bfloat16), -1)
    rank = jnp.dot(earlier, mask.astype(jnp.bfloat16), preferred_element_type=jnp.float32)
    rank = jnp.where(mask, rank.astype(jnp.int32), -1)
    in_slot = rank[:, :, None] == jnp.arange(CAP, dtype=jnp.int32)
    place = in_slot.reshape(tok_dev, slot_total).astype(jnp.bfloat16)
    gate_hi = gate_of.astype(jnp.bfloat16)
    gate_lo = (gate_of - gate_hi.astype(jnp.float32)).astype(jnp.bfloat16)
    weigh = jnp.concatenate(
        [
            jnp.where(in_slot, part[:, :, None], 0.0).astype(jnp.bfloat16).reshape(tok_dev, slot_total)
            for part in (gate_hi, gate_lo)
        ],
        axis=0,
    )

    send = lax.dot_general(place, tokens, (((0,), (0,)), ((), ())), preferred_element_type=jnp.float32)
    send = send.astype(jnp.bfloat16).reshape(ep_count, CAP, width)
    rows = lax.all_to_all(send, "ep", split_axis=0, concat_axis=0, tiled=True).reshape(slot_total, width)

    total = None
    for steps in GROUPS_OF_STEPS:
        total = up_step(
            here.reshape(1), rows, [up[step] for step in steps], total, steps, steps == GROUPS_OF_STEPS[-1]
        )
    hidden = total

    half = width // size // 2
    out = jnp.zeros((tok_dev, width), jnp.bfloat16)
    for steps in GROUPS_OF_STEPS:
        answer = down_step(hidden, [down[step] for step in steps])
        part = answer.shape[1]
        back = lax.all_to_all(
            answer.reshape(ep_count, CAP, part), "ep", split_axis=0, concat_axis=0, tiled=True
        ).reshape(slot_total, part)
        both = jnp.dot(weigh, back, preferred_element_type=jnp.float32)
        mixed = (both[:tok_dev] + both[tok_dev:]).astype(jnp.bfloat16)
        for turn, step in enumerate(steps):
            for side, sign in enumerate((-1, 1)):
                start = (2 * turn + side) * half
                source = lax.rem(here + sign * step + size, size)
                out = lax.dynamic_update_slice(
                    out, mixed[:, start:start + half], (0, (2 * source + side) * half)
                )
    return out[None, None]


def solution(mesh):
    placed = (
        P("grp", None, "ep", None),
        P("grp", None, "ep", None),
        P("grp", None, None, None),
        P("ep", "grp", None),
        P("ep", None, "grp"),
    )
    return jax.shard_map(
        local, mesh=mesh, in_specs=placed, out_specs=P("grp", None, "ep", None), check_vma=False
    )
```

```python
import jax
import jax.numpy as jnp
from jax import lax
from jax.experimental import pallas as pl
from jax.experimental.pallas import tpu as pltpu
from jax.sharding import PartitionSpec as P

E = 32
BLK = 128
CAP = 16
UP_GROUPS = ((0, 1, 2, 3), (4, 5), (6, 7))
DOWN_GROUPS = ((0, 1), (2, 3), (4, 5), (6, 7))
LIGHT = pl.CostEstimate(flops=2_000_000_000, bytes_accessed=4_000_000, transcendentals=0)
VMEM = 56 * 1024 * 1024
UNREAD = pl.BlockSpec(memory_space=pl.ANY)


def coded_block(entries):
    largest = jnp.max(jnp.max(jnp.abs(entries), axis=0, keepdims=True), axis=1, keepdims=True)
    scale = (largest / 448.0 + 1e-06).astype(jnp.bfloat16).astype(jnp.float32)
    coded = (entries / scale).astype(jnp.bfloat16)
    return (coded.astype(jnp.float32) * scale).astype(jnp.bfloat16)


def requantize_kernel(master_ref, *refs):
    out_refs = refs[-2:]
    width = out_refs[0].shape[1]
    for column in range(0, master_ref.shape[1], BLK):
        place = column % width
        for row in range(0, master_ref.shape[0], BLK):
            out_refs[column // width][row:row + BLK, place:place + BLK] = coded_block(
                master_ref[row:row + BLK, column:column + BLK]
            )


def requantize(master, step, name, after=()):
    height, width = master.shape
    return pl.pallas_call(
        requantize_kernel,
        grid=(height // step,),
        in_specs=[pl.BlockSpec((step, width), lambda i: (i, 0))] + [UNREAD] * len(after),
        out_specs=[pl.BlockSpec((step, width // 2), lambda i: (i, 0))] * 2,
        out_shape=[jax.ShapeDtypeStruct((height, width // 2), jnp.bfloat16)] * 2,
        cost_estimate=LIGHT,
        name=name,
    )(master, *after)


def silu(total):
    return total / (1.0 + jnp.exp(-total))


def up_kernel(steps, size, place_ref, *refs):
    out_ref = refs[-1]
    count = 2 * len(steps)
    rows, weights = refs[:count], refs[count:2 * count]
    part = weights[0].shape[1]
    for side in range(2):
        place = slice(side * part, (side + 1) * part)
        total = None if steps[0] == 0 else refs[2 * count][:, place]
        for index in range(side, count, 2):
            product = jnp.dot(
                rows[index][...], weights[index][...], preferred_element_type=jnp.float32
            )
            total = product if total is None else total + product
        if steps[-1] == size - 1:
            total = silu(total)
        out_ref[:, place] = total.astype(out_ref.dtype)


def up_step(here, rows, slices, total, steps, size, after=()):
    parts = [part for one in slices for part in one]
    if total is not None:
        parts.append(total)
    count, depth = rows.shape[0], rows.shape[1] // size
    width = 2 * parts[0].shape[1]
    last = steps[-1] == size - 1
    whole = lambda shape: pl.BlockSpec(shape, lambda i, place: (0, 0))
    block = lambda offset: pl.BlockSpec(
        (count, depth), lambda i, place: (0, lax.rem(place[0] + offset, size))
    )
    blocks = [block(size + sign * step) for step in steps for sign in (-1, 1)]
    return pl.pallas_call(
        lambda *refs: up_kernel(steps, size, *refs),
        grid_spec=pltpu.PrefetchScalarGridSpec(
            num_scalar_prefetch=1,
            grid=(1,),
            in_specs=blocks + [whole(part.shape) for part in parts] + [UNREAD] * len(after),
            out_specs=whole((count, width)),
        ),
        out_shape=jax.ShapeDtypeStruct((count, width), jnp.bfloat16 if last else jnp.float32),
        compiler_params=pltpu.CompilerParams(vmem_limit_bytes=VMEM),
        cost_estimate=LIGHT,
        name="up_step",
    )(here.reshape(1), *[rows] * len(blocks), *parts, *after)


def down_kernel(count, hidden_ref, *refs):
    out_ref = refs[-1]
    part = refs[0].shape[1]
    for index in range(count):
        out_ref[:, index * part:(index + 1) * part] = jnp.dot(
            hidden_ref[...], refs[index][...], preferred_element_type=jnp.float32
        ).astype(out_ref.dtype)


def down_step(hidden, slices, after=()):
    parts = [part for one in slices for part in one]
    count = hidden.shape[0]
    width = sum(part.shape[1] for part in parts)
    whole = lambda shape: pl.BlockSpec(shape, lambda i: (0, 0))
    return pl.pallas_call(
        lambda *refs: down_kernel(len(parts), *refs),
        grid=(1,),
        in_specs=[whole(part.shape) for part in (hidden, *parts)] + [UNREAD] * len(after),
        out_specs=whole((count, width)),
        out_shape=jax.ShapeDtypeStruct((count, width), jnp.bfloat16),
        compiler_params=pltpu.CompilerParams(vmem_limit_bytes=VMEM),
        cost_estimate=LIGHT,
        name="down_step",
    )(hidden, *parts, *after)


def wait_for(parts, after):
    return [lax.optimization_barrier((part, *after))[0] for part in parts] if after else parts


def shift(parts):
    size = lax.axis_size("grp")
    right = [(i, (i + 1) % size) for i in range(size)]
    left = [(i, (i - 1) % size) for i in range(size)]
    return [lax.ppermute(part, "grp", way) for part, way in zip(parts, (right, left))]


def advance(held, *beside):
    now, beside = lax.optimization_barrier((shift(held[-1]), beside))
    held.append(now)
    return beside


def local(tokens, gates, routes, master_up, master_down):
    tokens = tokens[0, 0]
    gates = gates[0, 0]
    routes = routes[0, 0]
    ep_count = lax.axis_size("ep")
    size = lax.axis_size("grp")
    tok_dev, width = tokens.shape
    slot_total = ep_count * CAP
    here = lax.axis_index("grp").astype(jnp.int32)

    everyone = lax.all_gather(tokens, "ep", axis=0, tiled=True)

    up = [requantize(master_up[0], BLK, "requantize_up")]
    advance(up)

    own_routes = lax.dynamic_slice_in_dim(routes, lax.axis_index("ep") * tok_dev, tok_dev, 0)
    named = own_routes[:, :, None] == jnp.arange(E, dtype=jnp.int32)
    mask = jnp.any(named, axis=1)
    gate_of = jnp.sum(jnp.where(named, gates[:, :, None], 0.0), axis=1)
    earlier = jnp.tril(jnp.ones((tok_dev, tok_dev), jnp.bfloat16), -1)
    rank = jnp.dot(earlier, mask.astype(jnp.bfloat16), preferred_element_type=jnp.float32)
    rank = jnp.where(mask, rank.astype(jnp.int32), -1)
    in_slot = rank[:, :, None] == jnp.arange(CAP, dtype=jnp.int32)
    gate_hi = gate_of.astype(jnp.bfloat16)
    gate_lo = (gate_of - gate_hi.astype(jnp.float32)).astype(jnp.bfloat16)
    weigh = jnp.concatenate(
        [
            jnp.where(in_slot, part[:, :, None], 0.0).astype(jnp.bfloat16).reshape(tok_dev, slot_total)
            for part in (gate_hi, gate_lo)
        ],
        axis=0,
    )

    own = lax.axis_index("ep").astype(jnp.int32)
    asks = jnp.any(routes == own, axis=1).reshape(ep_count, tok_dev)
    ahead = jnp.triu(jnp.ones((tok_dev, tok_dev), jnp.bfloat16), 1)
    slot = jnp.dot(asks.astype(jnp.bfloat16), ahead, preferred_element_type=jnp.float32)
    slot = slot.astype(jnp.int32) + CAP * jnp.arange(ep_count, dtype=jnp.int32)[:, None]
    slot = jnp.where(asks, slot, -1).reshape(1, ep_count * tok_dev)
    take = (slot == jnp.arange(slot_total, dtype=jnp.int32)[:, None]).astype(jnp.bfloat16)

    down = [requantize(master_down[0], 3 * BLK, "requantize_down", up[1][:1])]
    (down[0],) = advance(up, down[0])
    advance(up)
    advance(up)
    rows = jnp.dot(
        wait_for([take], up[4][:1])[0], everyone, preferred_element_type=jnp.float32
    ).astype(jnp.bfloat16)
    (rows,) = advance(up, rows)

    def send_back(answer):
        part = answer.shape[1]
        return lax.all_to_all(
            answer.reshape(ep_count, CAP, part), "ep", split_axis=0, concat_axis=0, tiled=True
        ).reshape(slot_total, part)

    def mix(back, after):
        both = jnp.dot(wait_for([weigh], after)[0], back, preferred_element_type=jnp.float32)
        return (both[:tok_dev] + both[tok_dev:]).astype(jnp.bfloat16)

    def add_up(steps, total):
        return up_step(here, rows, [up[step] for step in steps], total, steps, size)

    def answers(steps):
        return down_step(hidden, [down[step] for step in steps])

    (total,) = advance(up, add_up(UP_GROUPS[0], None))
    total, down[0] = advance(up, add_up(UP_GROUPS[1], total), down[0])
    (hidden,) = advance(down, add_up(UP_GROUPS[2], total))
    (first,) = advance(down, answers(DOWN_GROUPS[0]))
    back = send_back(first)
    advance(down)
    second, back = advance(down, answers(DOWN_GROUPS[1]), back)
    backs = [back]
    back = send_back(second)
    advance(down)
    third, back = advance(down, answers(DOWN_GROUPS[2]), back)
    backs.append(back)
    backs.append(send_back(third))
    advance(down)
    backs.append(send_back(answers(DOWN_GROUPS[3])))
    mixed = [mix(back, ()) for back in backs]

    half = width // size // 2
    out = jnp.zeros((tok_dev, width), jnp.bfloat16)
    for steps, piece in zip(DOWN_GROUPS, mixed):
        for turn, step in enumerate(steps):
            for side, sign in enumerate((-1, 1)):
                start = (2 * turn + side) * half
                source = lax.rem(here + sign * step + size, size)
                out = lax.dynamic_update_slice(
                    out, piece[:, start:start + half], (0, (2 * source + side) * half)
                )
    return out[None, None]


def solution(mesh):
    placed = (
        P("grp", None, "ep", None),
        P("grp", None, "ep", None),
        P("grp", None, None, None),
        P("ep", "grp", None),
        P("ep", None, "grp"),
    )
    return jax.shard_map(
        local, mesh=mesh, in_specs=placed, out_specs=P("grp", None, "ep", None), check_vma=False
    )
```

```python
import jax
import jax.numpy as jnp
from jax import lax
from jax.experimental import pallas as pl
from jax.experimental.pallas import tpu as pltpu
from jax.sharding import PartitionSpec as P

E = 32
BLK = 128
CAP = 16
UP_GROUPS = ((0, 1, 2, 3), (4, 5), (6, 7))
DOWN_GROUPS = ((0, 1), (2, 3), (4, 5), (6, 7))
LIGHT = pl.CostEstimate(flops=2_000_000_000, bytes_accessed=4_000_000, transcendentals=0)
TILE = 256
VMEM = 56 * 1024 * 1024
UNREAD = pl.BlockSpec(memory_space=pl.ANY)


def coded_block(entries):
    largest = jnp.max(jnp.max(jnp.abs(entries), axis=0, keepdims=True), axis=1, keepdims=True)
    scale = (largest / 448.0 + 1e-06).astype(jnp.bfloat16).astype(jnp.float32)
    coded = (entries / scale).astype(jnp.bfloat16)
    return (coded.astype(jnp.float32) * scale).astype(jnp.bfloat16)


def requantize_kernel(master_ref, *refs):
    out_refs = refs[-2:]
    width = out_refs[0].shape[1]
    for column in range(0, master_ref.shape[1], BLK):
        place = column % width
        for row in range(0, master_ref.shape[0], BLK):
            out_refs[column // width][row:row + BLK, place:place + BLK] = coded_block(
                master_ref[row:row + BLK, column:column + BLK]
            )


def requantize(master, step, name, after=()):
    height, width = master.shape
    return pl.pallas_call(
        requantize_kernel,
        grid=(height // step,),
        in_specs=[pl.BlockSpec((step, width), lambda i: (i, 0))] + [UNREAD] * len(after),
        out_specs=[pl.BlockSpec((step, width // 2), lambda i: (i, 0))] * 2,
        out_shape=[jax.ShapeDtypeStruct((height, width // 2), jnp.bfloat16)] * 2,
        cost_estimate=LIGHT,
        name=name,
    )(master, *after)


def silu(total):
    return total / (1.0 + jnp.exp(-total))


def up_kernel(steps, size, place_ref, *refs):
    out_ref = refs[-1]
    count = 2 * len(steps)
    rows, weights = refs[:count], refs[count:2 * count]
    part = weights[0].shape[1]
    for side in range(2):

        @pl.loop(0, part // TILE)
        def _(tile, side=side):
            columns = pl.ds(pl.multiple_of(tile * TILE, TILE), TILE)
            place = pl.ds(pl.multiple_of(side * part + tile * TILE, TILE), TILE)
            total = None if steps[0] == 0 else refs[2 * count][:, place]
            for index in range(side, count, 2):
                product = jnp.dot(
                    rows[index][...], weights[index][:, columns], preferred_element_type=jnp.float32
                )
                total = product if total is None else total + product
            if steps[-1] == size - 1:
                total = silu(total)
            out_ref[:, place] = total.astype(out_ref.dtype)


def up_step(here, rows, slices, total, steps, size, after=()):
    parts = [part for one in slices for part in one]
    if total is not None:
        parts.append(total)
    count, depth = rows.shape[0], rows.shape[1] // size
    width = 2 * parts[0].shape[1]
    last = steps[-1] == size - 1
    whole = lambda shape: pl.BlockSpec(shape, lambda i, place: (0, 0))
    block = lambda offset: pl.BlockSpec(
        (count, depth), lambda i, place: (0, lax.rem(place[0] + offset, size))
    )
    blocks = [block(size + sign * step) for step in steps for sign in (-1, 1)]
    return pl.pallas_call(
        lambda *refs: up_kernel(steps, size, *refs),
        grid_spec=pltpu.PrefetchScalarGridSpec(
            num_scalar_prefetch=1,
            grid=(1,),
            in_specs=blocks + [whole(part.shape) for part in parts] + [UNREAD] * len(after),
            out_specs=whole((count, width)),
        ),
        out_shape=jax.ShapeDtypeStruct((count, width), jnp.bfloat16 if last else jnp.float32),
        compiler_params=pltpu.CompilerParams(vmem_limit_bytes=VMEM),
        cost_estimate=LIGHT,
        name="up_step",
    )(here.reshape(1), *[rows] * len(blocks), *parts, *after)


def down_kernel(count, hidden_ref, *refs):
    out_ref = refs[-1]
    part = refs[0].shape[1]

    @pl.loop(0, hidden_ref.shape[0] // TILE)
    def _(tile):
        rows = pl.ds(pl.multiple_of(tile * TILE, TILE), TILE)
        for index in range(count):
            out_ref[rows, index * part:(index + 1) * part] = jnp.dot(
                hidden_ref[rows, :], refs[index][...], preferred_element_type=jnp.float32
            ).astype(out_ref.dtype)


def down_step(hidden, slices, after=()):
    parts = [part for one in slices for part in one]
    count = hidden.shape[0]
    width = sum(part.shape[1] for part in parts)
    whole = lambda shape: pl.BlockSpec(shape, lambda i: (0, 0))
    return pl.pallas_call(
        lambda *refs: down_kernel(len(parts), *refs),
        grid=(1,),
        in_specs=[whole(part.shape) for part in (hidden, *parts)] + [UNREAD] * len(after),
        out_specs=whole((count, width)),
        out_shape=jax.ShapeDtypeStruct((count, width), jnp.bfloat16),
        compiler_params=pltpu.CompilerParams(vmem_limit_bytes=VMEM),
        cost_estimate=LIGHT,
        name="down_step",
    )(hidden, *parts, *after)


def shift(parts):
    size = lax.axis_size("grp")
    right = [(i, (i + 1) % size) for i in range(size)]
    left = [(i, (i - 1) % size) for i in range(size)]
    return [lax.ppermute(part, "grp", way) for part, way in zip(parts, (right, left))]


def advance(held, *beside):
    now, beside = lax.optimization_barrier((shift(held[-1]), beside))
    held.append(now)
    return beside


def local(tokens, gates, routes, master_up, master_down):
    tokens = tokens[0, 0]
    gates = gates[0, 0]
    routes = routes[0, 0]
    ep_count = lax.axis_size("ep")
    size = lax.axis_size("grp")
    tok_dev, width = tokens.shape
    slot_total = ep_count * CAP
    here = lax.axis_index("grp").astype(jnp.int32)

    own_routes = lax.dynamic_slice_in_dim(routes, lax.axis_index("ep") * tok_dev, tok_dev, 0)
    named = own_routes[:, :, None] == jnp.arange(E, dtype=jnp.int32)
    mask = jnp.any(named, axis=1)
    gate_of = jnp.sum(jnp.where(named, gates[:, :, None], 0.0), axis=1)
    earlier = jnp.tril(jnp.ones((tok_dev, tok_dev), jnp.bfloat16), -1)
    rank = jnp.dot(earlier, mask.astype(jnp.bfloat16), preferred_element_type=jnp.float32)
    rank = jnp.where(mask, rank.astype(jnp.int32), -1)
    in_slot = rank[:, :, None] == jnp.arange(CAP, dtype=jnp.int32)
    place = in_slot.reshape(tok_dev, slot_total).astype(jnp.bfloat16)
    gate_hi = gate_of.astype(jnp.bfloat16)
    gate_lo = (gate_of - gate_hi.astype(jnp.float32)).astype(jnp.bfloat16)
    weigh = jnp.concatenate(
        [
            jnp.where(in_slot, part[:, :, None], 0.0).astype(jnp.bfloat16).reshape(tok_dev, slot_total)
            for part in (gate_hi, gate_lo)
        ],
        axis=0,
    )

    up = [requantize(master_up[0], BLK, "requantize_up")]
    send = lax.dot_general(place, tokens, (((0,), (0,)), ((), ())), preferred_element_type=jnp.float32)
    send = send.astype(jnp.bfloat16).reshape(ep_count, CAP, width)
    advance(up)
    rows = lax.all_to_all(send, "ep", split_axis=0, concat_axis=0, tiled=True).reshape(slot_total, width)
    advance(up)
    down = [requantize(master_down[0], 3 * BLK, "requantize_down", up[2][:1])]
    (down[0],) = advance(up, down[0])
    advance(up)
    (rows,) = advance(up, rows)

    def send_back(answer):
        part = answer.shape[1]
        return lax.all_to_all(
            answer.reshape(ep_count, CAP, part), "ep", split_axis=0, concat_axis=0, tiled=True
        ).reshape(slot_total, part)

    def mix(back):
        both = jnp.dot(weigh, back, preferred_element_type=jnp.float32)
        return (both[:tok_dev] + both[tok_dev:]).astype(jnp.bfloat16)

    def add_up(steps, total):
        return up_step(here, rows, [up[step] for step in steps], total, steps, size)

    def answers(steps):
        return down_step(hidden, [down[step] for step in steps])

    (total,) = advance(up, add_up(UP_GROUPS[0], None))
    total, down[0] = advance(up, add_up(UP_GROUPS[1], total), down[0])
    (hidden,) = advance(down, add_up(UP_GROUPS[2], total))
    (first,) = advance(down, answers(DOWN_GROUPS[0]))
    back = send_back(first)
    advance(down)
    second, back = advance(down, answers(DOWN_GROUPS[1]), back)
    backs = [back]
    back = send_back(second)
    advance(down)
    third = answers(DOWN_GROUPS[2])
    last = send_back(third)
    third, back = advance(down, third, back)
    backs += [back, last]
    advance(down)
    backs.append(send_back(answers(DOWN_GROUPS[3])))
    mixed = [mix(back) for back in backs]

    half = width // size // 2
    out = jnp.zeros((tok_dev, width), jnp.bfloat16)
    for steps, piece in zip(DOWN_GROUPS, mixed):
        for turn, step in enumerate(steps):
            for side, sign in enumerate((-1, 1)):
                start = (2 * turn + side) * half
                source = lax.rem(here + sign * step + size, size)
                out = lax.dynamic_update_slice(
                    out, piece[:, start:start + half], (0, (2 * source + side) * half)
                )
    return out[None, None]


def solution(mesh):
    placed = (
        P("grp", None, "ep", None),
        P("grp", None, "ep", None),
        P("grp", None, None, None),
        P("ep", "grp", None),
        P("ep", None, "grp"),
    )
    return jax.shard_map(
        local, mesh=mesh, in_specs=placed, out_specs=P("grp", None, "ep", None), check_vma=False
    )
```

```python
import jax
import jax.numpy as jnp
from jax import lax
from jax.experimental import pallas as pl
from jax.experimental.pallas import tpu as pltpu
from jax.sharding import PartitionSpec as P

E = 32
BLK = 128
CAP = 16
UP_GROUPS = ((0, 1, 2, 3), (4, 5), (6, 7))
DOWN_GROUPS = ((0, 1), (2, 3), (4, 5), (6, 7))
LIGHT = pl.CostEstimate(flops=2_000_000_000, bytes_accessed=4_000_000, transcendentals=0)
TILE = 256
CUTS = 4
VMEM = 56 * 1024 * 1024
UNREAD = pl.BlockSpec(memory_space=pl.ANY)


def requantize_kernel(*refs):
    master_refs, out_refs = refs[:CUTS], refs[-2:]
    height, part = master_refs[0].shape
    share = out_refs[0].shape[1]
    blocks = [
        (cut, row, column)
        for cut in range(CUTS)
        for row in range(0, height, BLK)
        for column in range(0, part, BLK)
    ]
    entries = lambda cut, row, column: master_refs[cut][row:row + BLK, column:column + BLK]
    largest = [jnp.max(jnp.abs(entries(*block)), axis=0, keepdims=True) for block in blocks]
    largest = jnp.max(jnp.concatenate(largest, axis=0), axis=1, keepdims=True)
    scales = (largest / 448.0 + 1e-06).astype(jnp.bfloat16).astype(jnp.float32)
    for index, (cut, row, column) in enumerate(blocks):
        scale = scales[index:index + 1, :]
        coded = (entries(cut, row, column) / scale).astype(jnp.bfloat16)
        side, place = divmod(cut * part + column, share)
        out_refs[side][row:row + BLK, place:place + BLK] = (
            coded.astype(jnp.float32) * scale
        ).astype(jnp.bfloat16)


def requantize(master, step, name, after=()):
    height, width = master.shape
    cuts = [pl.BlockSpec((step, width // CUTS), lambda i, cut=cut: (i, cut)) for cut in range(CUTS)]
    return pl.pallas_call(
        requantize_kernel,
        grid=(height // step,),
        in_specs=cuts + [UNREAD] * len(after),
        out_specs=[pl.BlockSpec((step, width // 2), lambda i: (i, 0))] * 2,
        out_shape=[jax.ShapeDtypeStruct((height, width // 2), jnp.bfloat16)] * 2,
        cost_estimate=LIGHT,
        name=name,
    )(*[master] * CUTS, *after)


def silu(total):
    return total / (1.0 + jnp.exp(-total))


def up_kernel(steps, size, place_ref, *refs):
    out_ref = refs[-1]
    count = 2 * len(steps)
    rows, weights = refs[:count], refs[count:2 * count]
    part = weights[0].shape[1]
    for side in range(2):

        @pl.loop(0, part // TILE)
        def _(tile, side=side):
            columns = pl.ds(pl.multiple_of(tile * TILE, TILE), TILE)
            place = pl.ds(pl.multiple_of(side * part + tile * TILE, TILE), TILE)
            total = None if steps[0] == 0 else refs[2 * count][:, place]
            for index in range(side, count, 2):
                product = jnp.dot(
                    rows[index][...], weights[index][:, columns], preferred_element_type=jnp.float32
                )
                total = product if total is None else total + product
            if steps[-1] == size - 1:
                total = silu(total)
            out_ref[:, place] = total.astype(out_ref.dtype)


def up_step(here, rows, slices, total, steps, size, after=()):
    parts = [part for one in slices for part in one]
    if total is not None:
        parts.append(total)
    count, depth = rows.shape[0], rows.shape[1] // size
    width = 2 * parts[0].shape[1]
    last = steps[-1] == size - 1
    whole = lambda shape: pl.BlockSpec(shape, lambda i, place: (0, 0))
    block = lambda offset: pl.BlockSpec(
        (count, depth), lambda i, place: (0, lax.rem(place[0] + offset, size))
    )
    blocks = [block(size + sign * step) for step in steps for sign in (-1, 1)]
    return pl.pallas_call(
        lambda *refs: up_kernel(steps, size, *refs),
        grid_spec=pltpu.PrefetchScalarGridSpec(
            num_scalar_prefetch=1,
            grid=(1,),
            in_specs=blocks + [whole(part.shape) for part in parts] + [UNREAD] * len(after),
            out_specs=whole((count, width)),
        ),
        out_shape=jax.ShapeDtypeStruct((count, width), jnp.bfloat16 if last else jnp.float32),
        compiler_params=pltpu.CompilerParams(vmem_limit_bytes=VMEM),
        cost_estimate=LIGHT,
        name="up_step",
    )(here.reshape(1), *[rows] * len(blocks), *parts, *after)


def down_kernel(count, hidden_ref, *refs):
    out_ref = refs[-1]
    part = refs[0].shape[1]

    @pl.loop(0, hidden_ref.shape[0] // TILE)
    def _(tile):
        rows = pl.ds(pl.multiple_of(tile * TILE, TILE), TILE)
        for index in range(count):
            out_ref[rows, index * part:(index + 1) * part] = jnp.dot(
                hidden_ref[rows, :], refs[index][...], preferred_element_type=jnp.float32
            ).astype(out_ref.dtype)


def down_step(hidden, slices, groups=1, buffer=None):
    parts = [part for one in slices for part in one]
    count = hidden.shape[0]
    width = sum(part.shape[1] for part in parts)
    whole = lambda shape: pl.BlockSpec(shape, lambda i: (0, 0))
    given = [] if buffer is None else [buffer]
    second = len(given)
    return pl.pallas_call(
        lambda *refs: down_kernel(len(parts), *refs),
        grid=(1,),
        in_specs=[whole(part.shape) for part in (hidden, *parts)] + [UNREAD] * second,
        out_specs=pl.BlockSpec((count, width), lambda i: (0, second)),
        out_shape=jax.ShapeDtypeStruct((count, width * groups), jnp.bfloat16),
        input_output_aliases={1 + len(parts): 0} if second else {},
        compiler_params=pltpu.CompilerParams(vmem_limit_bytes=VMEM),
        cost_estimate=LIGHT,
        name="down_step",
    )(hidden, *parts, *given)


def shift(parts):
    size = lax.axis_size("grp")
    right = [(i, (i + 1) % size) for i in range(size)]
    left = [(i, (i - 1) % size) for i in range(size)]
    return [lax.ppermute(part, "grp", way) for part, way in zip(parts, (right, left))]


def advance(held, *beside):
    now, beside = lax.optimization_barrier((shift(held[-1]), beside))
    held.append(now)
    return beside


def local(tokens, gates, routes, master_up, master_down):
    tokens = tokens[0, 0]
    gates = gates[0, 0]
    routes = routes[0, 0]
    ep_count = lax.axis_size("ep")
    size = lax.axis_size("grp")
    tok_dev, width = tokens.shape
    slot_total = ep_count * CAP
    here = lax.axis_index("grp").astype(jnp.int32)

    own_routes = lax.dynamic_slice_in_dim(routes, lax.axis_index("ep") * tok_dev, tok_dev, 0)
    named = own_routes[:, :, None] == jnp.arange(E, dtype=jnp.int32)
    mask = jnp.any(named, axis=1)
    gate_of = jnp.sum(jnp.where(named, gates[:, :, None], 0.0), axis=1)
    earlier = jnp.tril(jnp.ones((tok_dev, tok_dev), jnp.bfloat16), -1)
    rank = jnp.dot(earlier, mask.astype(jnp.bfloat16), preferred_element_type=jnp.float32)
    rank = jnp.where(mask, rank.astype(jnp.int32), -1)
    in_slot = rank[:, :, None] == jnp.arange(CAP, dtype=jnp.int32)
    place = in_slot.reshape(tok_dev, slot_total).astype(jnp.bfloat16)
    gate_hi = gate_of.astype(jnp.bfloat16)
    gate_lo = (gate_of - gate_hi.astype(jnp.float32)).astype(jnp.bfloat16)
    weigh = jnp.concatenate(
        [
            jnp.where(in_slot, part[:, :, None], 0.0).astype(jnp.bfloat16).reshape(tok_dev, slot_total)
            for part in (gate_hi, gate_lo)
        ],
        axis=0,
    )

    up = [requantize(master_up[0], BLK, "requantize_up")]
    send = lax.dot_general(place, tokens, (((0,), (0,)), ((), ())), preferred_element_type=jnp.float32)
    send = send.astype(jnp.bfloat16).reshape(ep_count, CAP, width)
    advance(up)
    rows = lax.all_to_all(send, "ep", split_axis=0, concat_axis=0, tiled=True).reshape(slot_total, width)
    advance(up)
    down = [requantize(master_down[0], 3 * BLK, "requantize_down", up[2][:1])]
    (down[0],) = advance(up, down[0])
    advance(up)
    (rows,) = advance(up, rows)

    def send_back(answer):
        part = answer.shape[1]
        return lax.all_to_all(
            answer.reshape(ep_count, CAP, part), "ep", split_axis=0, concat_axis=0, tiled=True
        ).reshape(slot_total, part)

    def mix(back):
        both = jnp.dot(weigh, back, preferred_element_type=jnp.float32)
        return (both[:tok_dev] + both[tok_dev:]).astype(jnp.bfloat16)

    def add_up(steps, total):
        return up_step(here, rows, [up[step] for step in steps], total, steps, size)

    def answers(steps, groups=1, buffer=None):
        return down_step(hidden, [down[step] for step in steps], groups, buffer)

    (total,) = advance(up, add_up(UP_GROUPS[0], None))
    total, down[0] = advance(up, add_up(UP_GROUPS[1], total), down[0])
    (hidden,) = advance(down, add_up(UP_GROUPS[2], total))
    (first,) = advance(down, answers(DOWN_GROUPS[0]))
    back = send_back(first)
    advance(down)
    second, back = advance(down, answers(DOWN_GROUPS[1]), back)
    backs = [back]
    back = send_back(second)
    advance(down)
    third = answers(DOWN_GROUPS[2])
    last = send_back(third)
    third, back = advance(down, third, back)
    backs += [back, last]
    fourth = answers(DOWN_GROUPS[3][:1], 2)
    (fourth,) = advance(down, fourth)
    backs.append(send_back(answers(DOWN_GROUPS[3][1:], 2, fourth)))
    mixed = [mix(back) for back in backs]

    half = width // size // 2
    out = jnp.zeros((tok_dev, width), jnp.bfloat16)
    for steps, piece in zip(DOWN_GROUPS, mixed):
        for turn, step in enumerate(steps):
            for side, sign in enumerate((-1, 1)):
                start = (2 * turn + side) * half
                source = lax.rem(here + sign * step + size, size)
                out = lax.dynamic_update_slice(
                    out, piece[:, start:start + half], (0, (2 * source + side) * half)
                )
    return out[None, None]


def solution(mesh):
    placed = (
        P("grp", None, "ep", None),
        P("grp", None, "ep", None),
        P("grp", None, None, None),
        P("ep", "grp", None),
        P("ep", None, "grp"),
    )
    return jax.shard_map(
        local, mesh=mesh, in_specs=placed, out_specs=P("grp", None, "ep", None), check_vma=False
    )
```

```python
import jax
import jax.numpy as jnp
from jax import lax
from jax.experimental import pallas as pl
from jax.experimental.pallas import tpu as pltpu
from jax.sharding import PartitionSpec as P

E = 32
BLK = 128
CAP = 16
UP_GROUPS = ((0, 1, 2, 3), (4, 5), (6, 7))
DOWN_GROUPS = ((0, 1), (2, 3), (4, 5), (6, 7))
LIGHT = pl.CostEstimate(flops=2_000_000_000, bytes_accessed=4_000_000, transcendentals=0)
TILE = 256
CUTS = 4
VMEM = 56 * 1024 * 1024
UNREAD = pl.BlockSpec(memory_space=pl.ANY)


def requantize_kernel(*refs):
    master_refs, out_refs = refs[:CUTS], refs[-2:]
    height, part = master_refs[0].shape
    share = out_refs[0].shape[1]
    blocks = [
        (cut, row, column)
        for cut in range(CUTS)
        for row in range(0, height, BLK)
        for column in range(0, part, BLK)
    ]
    entries = lambda cut, row, column: master_refs[cut][row:row + BLK, column:column + BLK]
    largest = [jnp.max(jnp.abs(entries(*block)), axis=0, keepdims=True) for block in blocks]
    largest = jnp.max(jnp.concatenate(largest, axis=0), axis=1, keepdims=True)
    scales = (largest / 448.0 + 1e-06).astype(jnp.bfloat16).astype(jnp.float32)
    for index, (cut, row, column) in enumerate(blocks):
        scale = scales[index:index + 1, :]
        coded = (entries(cut, row, column) / scale).astype(jnp.bfloat16)
        side, place = divmod(cut * part + column, share)
        out_refs[side][row:row + BLK, place:place + BLK] = (
            coded.astype(jnp.float32) * scale
        ).astype(jnp.bfloat16)


def requantize(master, step, name, after=()):
    height, width = master.shape
    cuts = [pl.BlockSpec((step, width // CUTS), lambda i, cut=cut: (i, cut)) for cut in range(CUTS)]
    return pl.pallas_call(
        requantize_kernel,
        grid=(height // step,),
        in_specs=cuts + [UNREAD] * len(after),
        out_specs=[pl.BlockSpec((step, width // 2), lambda i: (i, 0))] * 2,
        out_shape=[jax.ShapeDtypeStruct((height, width // 2), jnp.bfloat16)] * 2,
        cost_estimate=LIGHT,
        name=name,
    )(*[master] * CUTS, *after)


def silu(total):
    return total / (1.0 + jnp.exp(-total))


def up_kernel(steps, size, place_ref, *refs):
    out_ref = refs[-1]
    count = 2 * len(steps)
    rows, weights = refs[:count], refs[count:2 * count]
    part = weights[0].shape[1]
    for side in range(2):

        @pl.loop(0, part // TILE)
        def _(tile, side=side):
            columns = pl.ds(pl.multiple_of(tile * TILE, TILE), TILE)
            place = pl.ds(pl.multiple_of(side * part + tile * TILE, TILE), TILE)
            total = None if steps[0] == 0 else refs[2 * count][:, place]
            for index in range(side, count, 2):
                product = jnp.dot(
                    rows[index][...], weights[index][:, columns], preferred_element_type=jnp.float32
                )
                total = product if total is None else total + product
            if steps[-1] == size - 1:
                total = silu(total)
            out_ref[:, place] = total.astype(out_ref.dtype)


def up_step(here, rows, slices, total, steps, size, after=()):
    parts = [part for one in slices for part in one]
    if total is not None:
        parts.append(total)
    count, depth = rows.shape[0], rows.shape[1] // size
    width = 2 * parts[0].shape[1]
    last = steps[-1] == size - 1
    whole = lambda shape: pl.BlockSpec(shape, lambda i, place: (0, 0))
    block = lambda offset: pl.BlockSpec(
        (count, depth), lambda i, place: (0, lax.rem(place[0] + offset, size))
    )
    blocks = [block(size + sign * step) for step in steps for sign in (-1, 1)]
    return pl.pallas_call(
        lambda *refs: up_kernel(steps, size, *refs),
        grid_spec=pltpu.PrefetchScalarGridSpec(
            num_scalar_prefetch=1,
            grid=(1,),
            in_specs=blocks + [whole(part.shape) for part in parts] + [UNREAD] * len(after),
            out_specs=whole((count, width)),
        ),
        out_shape=jax.ShapeDtypeStruct((count, width), jnp.bfloat16 if last else jnp.float32),
        compiler_params=pltpu.CompilerParams(vmem_limit_bytes=VMEM),
        cost_estimate=LIGHT,
        name="up_step",
    )(here.reshape(1), *[rows] * len(blocks), *parts, *after)


def down_kernel(count, hidden_ref, *refs):
    out_ref = refs[-1]
    part = refs[0].shape[1]

    @pl.loop(0, hidden_ref.shape[0] // TILE)
    def _(tile):
        rows = pl.ds(pl.multiple_of(tile * TILE, TILE), TILE)
        for index in range(count):
            out_ref[rows, index * part:(index + 1) * part] = jnp.dot(
                hidden_ref[rows, :], refs[index][...], preferred_element_type=jnp.float32
            ).astype(out_ref.dtype)


def down_step(hidden, slices, groups=1, buffer=None):
    parts = [part for one in slices for part in one]
    count = hidden.shape[0]
    width = sum(part.shape[1] for part in parts)
    whole = lambda shape: pl.BlockSpec(shape, lambda i: (0, 0))
    given = [] if buffer is None else [buffer]
    second = len(given)
    return pl.pallas_call(
        lambda *refs: down_kernel(len(parts), *refs),
        grid=(1,),
        in_specs=[whole(part.shape) for part in (hidden, *parts)] + [UNREAD] * second,
        out_specs=pl.BlockSpec((count, width), lambda i: (0, second)),
        out_shape=jax.ShapeDtypeStruct((count, width * groups), jnp.bfloat16),
        input_output_aliases={1 + len(parts): 0} if second else {},
        compiler_params=pltpu.CompilerParams(vmem_limit_bytes=VMEM),
        cost_estimate=LIGHT,
        name="down_step",
    )(hidden, *parts, *given)


def shift(parts):
    size = lax.axis_size("grp")
    right = [(i, (i + 1) % size) for i in range(size)]
    left = [(i, (i - 1) % size) for i in range(size)]
    return [lax.ppermute(part, "grp", way) for part, way in zip(parts, (right, left))]


def advance(held, *beside):
    now, beside = lax.optimization_barrier((shift(held[-1]), beside))
    held.append(now)
    return beside


def local(tokens, gates, routes, master_up, master_down):
    tokens = tokens[0, 0]
    gates = gates[0, 0]
    routes = routes[0, 0]
    ep_count = lax.axis_size("ep")
    size = lax.axis_size("grp")
    tok_dev, width = tokens.shape
    slot_total = ep_count * CAP
    here = lax.axis_index("grp").astype(jnp.int32)

    own_routes = lax.dynamic_slice_in_dim(routes, lax.axis_index("ep") * tok_dev, tok_dev, 0)
    named = own_routes[:, :, None] == jnp.arange(E, dtype=jnp.int32)
    mask = jnp.any(named, axis=1)
    gate_of = jnp.sum(jnp.where(named, gates[:, :, None], 0.0), axis=1)
    earlier = jnp.tril(jnp.ones((tok_dev, tok_dev), jnp.bfloat16), -1)
    rank = jnp.dot(earlier, mask.astype(jnp.bfloat16), preferred_element_type=jnp.float32)
    rank = jnp.where(mask, rank.astype(jnp.int32), -1)
    in_slot = rank[:, :, None] == jnp.arange(CAP, dtype=jnp.int32)
    place = in_slot.reshape(tok_dev, slot_total).astype(jnp.bfloat16)
    gate_hi = gate_of.astype(jnp.bfloat16)
    gate_lo = (gate_of - gate_hi.astype(jnp.float32)).astype(jnp.bfloat16)
    weigh = jnp.concatenate(
        [
            jnp.where(in_slot, part[:, :, None], 0.0).astype(jnp.bfloat16).reshape(tok_dev, slot_total)
            for part in (gate_hi, gate_lo)
        ],
        axis=0,
    )

    up = [requantize(master_up[0], 2 * BLK, "requantize_up")]
    send = lax.dot_general(place, tokens, (((0,), (0,)), ((), ())), preferred_element_type=jnp.float32)
    send = send.astype(jnp.bfloat16).reshape(ep_count, CAP, width)
    advance(up)
    rows = lax.all_to_all(send, "ep", split_axis=0, concat_axis=0, tiled=True).reshape(slot_total, width)
    advance(up)
    down = [requantize(master_down[0], 6 * BLK, "requantize_down", up[2][:1])]
    (down[0],) = advance(up, down[0])
    advance(up)
    (rows,) = advance(up, rows)

    def send_back(answer):
        part = answer.shape[1]
        return lax.all_to_all(
            answer.reshape(ep_count, CAP, part), "ep", split_axis=0, concat_axis=0, tiled=True
        ).reshape(slot_total, part)

    def mix(back):
        both = jnp.dot(weigh, back, preferred_element_type=jnp.float32)
        return (both[:tok_dev] + both[tok_dev:]).astype(jnp.bfloat16)

    def add_up(steps, total):
        return up_step(here, rows, [up[step] for step in steps], total, steps, size)

    def answers(steps, groups=1, buffer=None):
        return down_step(hidden, [down[step] for step in steps], groups, buffer)

    (total,) = advance(up, add_up(UP_GROUPS[0], None))
    total, down[0] = advance(up, add_up(UP_GROUPS[1], total), down[0])
    (hidden,) = advance(down, add_up(UP_GROUPS[2], total))
    (first,) = advance(down, answers(DOWN_GROUPS[0]))
    back = send_back(first)
    advance(down)
    second, back = advance(down, answers(DOWN_GROUPS[1]), back)
    backs = [back]
    back = send_back(second)
    advance(down)
    third = answers(DOWN_GROUPS[2])
    last = send_back(third)
    third, back = advance(down, third, back)
    backs += [back, last]
    fourth = answers(DOWN_GROUPS[3][:1], 2)
    (fourth,) = advance(down, fourth)
    backs.append(send_back(answers(DOWN_GROUPS[3][1:], 2, fourth)))
    mixed = [mix(back) for back in backs]

    half = width // size // 2
    out = jnp.zeros((tok_dev, width), jnp.bfloat16)
    for steps, piece in zip(DOWN_GROUPS, mixed):
        for turn, step in enumerate(steps):
            for side, sign in enumerate((-1, 1)):
                start = (2 * turn + side) * half
                source = lax.rem(here + sign * step + size, size)
                out = lax.dynamic_update_slice(
                    out, piece[:, start:start + half], (0, (2 * source + side) * half)
                )
    return out[None, None]


def solution(mesh):
    placed = (
        P("grp", None, "ep", None),
        P("grp", None, "ep", None),
        P("grp", None, None, None),
        P("ep", "grp", None),
        P("ep", None, "grp"),
    )
    return jax.shard_map(
        local, mesh=mesh, in_specs=placed, out_specs=P("grp", None, "ep", None), check_vma=False
    )
```

```python
import jax
import jax.numpy as jnp
from jax import lax
from jax.experimental import pallas as pl
from jax.experimental.pallas import tpu as pltpu
from jax.sharding import PartitionSpec as P

E = 32
BLK = 128
CAP = 16
UP_GROUPS = ((0, 1, 2, 3), (4, 5), (6, 7))
DOWN_GROUPS = ((0, 1), (2, 3), (4, 5), (6, 7))
LIGHT = pl.CostEstimate(flops=2_000_000_000, bytes_accessed=4_000_000, transcendentals=0)
TILE = 256
CUTS = 4
VMEM = 56 * 1024 * 1024
UNREAD = pl.BlockSpec(memory_space=pl.ANY)


def requantize_kernel(*refs):
    master_refs, out_refs = refs[:CUTS], refs[-2:]
    height, part = master_refs[0].shape
    share = out_refs[0].shape[1]
    blocks = [
        (cut, row, column)
        for cut in range(CUTS)
        for row in range(0, height, BLK)
        for column in range(0, part, BLK)
    ]
    entries = lambda cut, row, column: master_refs[cut][row:row + BLK, column:column + BLK]
    largest = [jnp.max(jnp.abs(entries(*block)), axis=0, keepdims=True) for block in blocks]
    largest = jnp.max(jnp.concatenate(largest, axis=0), axis=1, keepdims=True)
    scales = (largest / 448.0 + 1e-06).astype(jnp.bfloat16).astype(jnp.float32)
    for index, (cut, row, column) in enumerate(blocks):
        scale = scales[index:index + 1, :]
        coded = (entries(cut, row, column) / scale).astype(jnp.bfloat16)
        side, place = divmod(cut * part + column, share)
        out_refs[side][row:row + BLK, place:place + BLK] = (
            coded.astype(jnp.float32) * scale
        ).astype(jnp.bfloat16)


def requantize(master, step, name, after=()):
    height, width = master.shape
    cuts = [pl.BlockSpec((step, width // CUTS), lambda i, cut=cut: (i, cut)) for cut in range(CUTS)]
    return pl.pallas_call(
        requantize_kernel,
        grid=(height // step,),
        in_specs=cuts + [UNREAD] * len(after),
        out_specs=[pl.BlockSpec((step, width // 2), lambda i: (i, 0))] * 2,
        out_shape=[jax.ShapeDtypeStruct((height, width // 2), jnp.bfloat16)] * 2,
        cost_estimate=LIGHT,
        name=name,
    )(*[master] * CUTS, *after)


def silu(total):
    return total / (1.0 + jnp.exp(-total))


def up_kernel(steps, size, place_ref, *refs):
    out_ref = refs[-1]
    count = 2 * len(steps)
    rows, weights = refs[:count], refs[count:2 * count]
    part = weights[0].shape[1]
    for side in range(2):

        @pl.loop(0, part // TILE)
        def _(tile, side=side):
            columns = pl.ds(pl.multiple_of(tile * TILE, TILE), TILE)
            place = pl.ds(pl.multiple_of(side * part + tile * TILE, TILE), TILE)
            total = None if steps[0] == 0 else refs[2 * count][:, place]
            for index in range(side, count, 2):
                product = jnp.dot(
                    rows[index][...], weights[index][:, columns], preferred_element_type=jnp.float32
                )
                total = product if total is None else total + product
            if steps[-1] == size - 1:
                total = silu(total)
            out_ref[:, place] = total.astype(out_ref.dtype)


def up_step(here, rows, slices, total, steps, size, after=()):
    parts = [part for one in slices for part in one]
    if total is not None:
        parts.append(total)
    count, depth = rows.shape[0], rows.shape[1] // size
    width = 2 * parts[0].shape[1]
    last = steps[-1] == size - 1
    whole = lambda shape: pl.BlockSpec(shape, lambda i, place: (0, 0))
    block = lambda offset: pl.BlockSpec(
        (count, depth), lambda i, place: (0, lax.rem(place[0] + offset, size))
    )
    blocks = [block(size + sign * step) for step in steps for sign in (-1, 1)]
    return pl.pallas_call(
        lambda *refs: up_kernel(steps, size, *refs),
        grid_spec=pltpu.PrefetchScalarGridSpec(
            num_scalar_prefetch=1,
            grid=(1,),
            in_specs=blocks + [whole(part.shape) for part in parts] + [UNREAD] * len(after),
            out_specs=whole((count, width)),
        ),
        out_shape=jax.ShapeDtypeStruct((count, width), jnp.bfloat16 if last else jnp.float32),
        compiler_params=pltpu.CompilerParams(vmem_limit_bytes=VMEM),
        cost_estimate=LIGHT,
        name="up_step",
    )(here.reshape(1), *[rows] * len(blocks), *parts, *after)


def down_kernel(count, hidden_ref, *refs):
    out_ref = refs[-1]
    part = refs[0].shape[1]

    height = TILE if count > 2 else hidden_ref.shape[0]

    @pl.loop(0, hidden_ref.shape[0] // height)
    def _(tile):
        rows = pl.ds(pl.multiple_of(tile * height, height), height)
        for index in range(count):
            out_ref[rows, index * part:(index + 1) * part] = jnp.dot(
                hidden_ref[rows, :], refs[index][...], preferred_element_type=jnp.float32
            ).astype(out_ref.dtype)


def down_step(hidden, slices, groups=1, buffer=None):
    parts = [part for one in slices for part in one]
    count = hidden.shape[0]
    width = sum(part.shape[1] for part in parts)
    whole = lambda shape: pl.BlockSpec(shape, lambda i: (0, 0))
    given = [] if buffer is None else [buffer]
    second = len(given)
    return pl.pallas_call(
        lambda *refs: down_kernel(len(parts), *refs),
        grid=(1,),
        in_specs=[whole(part.shape) for part in (hidden, *parts)] + [UNREAD] * second,
        out_specs=pl.BlockSpec((count, width), lambda i: (0, second)),
        out_shape=jax.ShapeDtypeStruct((count, width * groups), jnp.bfloat16),
        input_output_aliases={1 + len(parts): 0} if second else {},
        compiler_params=pltpu.CompilerParams(vmem_limit_bytes=VMEM),
        cost_estimate=LIGHT,
        name="down_step",
    )(hidden, *parts, *given)


def shift(parts):
    size = lax.axis_size("grp")
    right = [(i, (i + 1) % size) for i in range(size)]
    left = [(i, (i - 1) % size) for i in range(size)]
    return [lax.ppermute(part, "grp", way) for part, way in zip(parts, (right, left))]


def advance(held, *beside):
    now, beside = lax.optimization_barrier((shift(held[-1]), beside))
    held.append(now)
    return beside


def local(tokens, gates, routes, master_up, master_down):
    tokens = tokens[0, 0]
    gates = gates[0, 0]
    routes = routes[0, 0]
    ep_count = lax.axis_size("ep")
    size = lax.axis_size("grp")
    tok_dev, width = tokens.shape
    slot_total = ep_count * CAP
    here = lax.axis_index("grp").astype(jnp.int32)

    own_routes = lax.dynamic_slice_in_dim(routes, lax.axis_index("ep") * tok_dev, tok_dev, 0)
    named = own_routes[:, :, None] == jnp.arange(E, dtype=jnp.int32)
    mask = jnp.any(named, axis=1)
    gate_of = jnp.sum(jnp.where(named, gates[:, :, None], 0.0), axis=1)
    earlier = jnp.tril(jnp.ones((tok_dev, tok_dev), jnp.bfloat16), -1)
    rank = jnp.dot(earlier, mask.astype(jnp.bfloat16), preferred_element_type=jnp.float32)
    rank = jnp.where(mask, rank.astype(jnp.int32), -1)
    in_slot = rank[:, :, None] == jnp.arange(CAP, dtype=jnp.int32)
    place = in_slot.reshape(tok_dev, slot_total).astype(jnp.bfloat16)
    gate_hi = gate_of.astype(jnp.bfloat16)
    gate_lo = (gate_of - gate_hi.astype(jnp.float32)).astype(jnp.bfloat16)
    weigh = jnp.concatenate(
        [
            jnp.where(in_slot, part[:, :, None], 0.0).astype(jnp.bfloat16).reshape(tok_dev, slot_total)
            for part in (gate_hi, gate_lo)
        ],
        axis=0,
    )

    up = [requantize(master_up[0], 2 * BLK, "requantize_up")]
    send = lax.dot_general(place, tokens, (((0,), (0,)), ((), ())), preferred_element_type=jnp.float32)
    send = send.astype(jnp.bfloat16).reshape(ep_count, CAP, width)
    advance(up)
    rows = lax.all_to_all(send, "ep", split_axis=0, concat_axis=0, tiled=True).reshape(slot_total, width)
    advance(up)
    down = [requantize(master_down[0], 6 * BLK, "requantize_down", up[2][:1])]
    (down[0],) = advance(up, down[0])
    advance(up)
    (rows,) = advance(up, rows)

    def send_back(answer):
        part = answer.shape[1]
        return lax.all_to_all(
            answer.reshape(ep_count, CAP, part), "ep", split_axis=0, concat_axis=0, tiled=True
        ).reshape(slot_total, part)

    def mix(back):
        both = jnp.dot(weigh, back, preferred_element_type=jnp.float32)
        return (both[:tok_dev] + both[tok_dev:]).astype(jnp.bfloat16)

    def add_up(steps, total):
        return up_step(here, rows, [up[step] for step in steps], total, steps, size)

    def answers(steps, groups=1, buffer=None):
        return down_step(hidden, [down[step] for step in steps], groups, buffer)

    (total,) = advance(up, add_up(UP_GROUPS[0], None))
    total, down[0] = advance(up, add_up(UP_GROUPS[1], total), down[0])
    (hidden,) = advance(down, add_up(UP_GROUPS[2], total))
    (first,) = advance(down, answers(DOWN_GROUPS[0]))
    back = send_back(first)
    advance(down)
    second, back = advance(down, answers(DOWN_GROUPS[1]), back)
    backs = [back]
    back = send_back(second)
    advance(down)
    third = answers(DOWN_GROUPS[2])
    last = send_back(third)
    third, back = advance(down, third, back)
    backs += [back, last]
    fourth = answers(DOWN_GROUPS[3][:1], 2)
    (fourth,) = advance(down, fourth)
    backs.append(send_back(answers(DOWN_GROUPS[3][1:], 2, fourth)))
    mixed = [mix(back) for back in backs]

    half = width // size // 2
    out = jnp.zeros((tok_dev, width), jnp.bfloat16)
    for steps, piece in zip(DOWN_GROUPS, mixed):
        for turn, step in enumerate(steps):
            for side, sign in enumerate((-1, 1)):
                start = (2 * turn + side) * half
                source = lax.rem(here + sign * step + size, size)
                out = lax.dynamic_update_slice(
                    out, piece[:, start:start + half], (0, (2 * source + side) * half)
                )
    return out[None, None]


def solution(mesh):
    placed = (
        P("grp", None, "ep", None),
        P("grp", None, "ep", None),
        P("grp", None, None, None),
        P("ep", "grp", None),
        P("ep", None, "grp"),
    )
    return jax.shard_map(
        local, mesh=mesh, in_specs=placed, out_specs=P("grp", None, "ep", None), check_vma=False
    )
```
